32 devices in a mesh: clips: 2 (over x), frames: 2 (over core), rows: 8 (over z, y).
Axes of the slice: x: 2, y: 2, z: 4, core: 2. Of those that a mesh axis runs over, the one named last changes fastest.
Arguments:
- noisy_video: bfloat16 [4, 64, 1024, 128], P(('clips', 'frames'), 'rows'), parts along dimension 0, may hold values from -60 to 60
- timestep: int32 [2], P('clips'), parts along dimension 0, may hold values from 100 to 899
- embed_weight: bfloat16 [512, 256], replicated, may hold values from -0.25 to 0.25
- norm_gain: float32 [2, 128], replicated, may hold values from 0.1 to 1.9
- norm_bias: float32 [2, 128], replicated, may hold values from -2.4 to 2.4
- conv_first: bfloat16 [3, 3, 128, 128], replicated, may hold values from -0.1875 to 0.1875
- temporal_weight: bfloat16 [3, 128, 128], replicated, may hold values from -0.3125 to 0.3125
- conv_second: bfloat16 [3, 3, 128, 128], replicated, may hold values from -0.1875 to 0.1875
Outputs:
- next_video: bfloat16 [4, 64, 1024, 128], P(('clips', 'frames'), 'rows'), parts along dimension 0
- predicted: float32 [4, 64, 1024, 128], P(('clips', 'frames'), 'rows'), parts along dimension 0
The draws below stay inside these ranges and needn't reach their ends.
There are 2 independent parts, one for each index of `clips`. The reference program is written for one: setup_inputs(seed, part) draws one part's arguments, and reference() takes and returns one part's arrays. A program takes and returns all parts, laid end to end along the dimension named above; an argument that names none is the same for every part. Nothing has to cross between parts.
All inputs are finite; a program needn't handle non-finite values.
Results may differ from the reference program's by a relative error of at most 0.002.
Values may be sent and summed in bfloat16 or wider, within the bound.
A program may use at most 128 MiB of HBM per device.

```python
import math
import jax
import jax.numpy as jnp
from jax import lax

CHANNELS = 128
GROUPS = 32
EMBED = 512
WIDTH_CELLS = 1024
TSTEPS = 1000
STRIDE = 8
FRAMES = 2
HEIGHT = 64


def draw_noisy_video(key, part):
    subkeys = jax.random.split(key, 3)
    full_shape = (FRAMES, HEIGHT, WIDTH_CELLS, CHANNELS)
    row_pos = jnp.arange(HEIGHT, dtype=jnp.float32)
    row_rise = 3.0 ** (row_pos / HEIGHT - 0.5)
    row_scale = jnp.exp(jax.random.uniform(subkeys[1], (HEIGHT,), jnp.float32, math.log(0.6), math.log(1.7)))
    col_scale = jnp.exp(jax.random.uniform(subkeys[2], (WIDTH_CELLS,), jnp.float32, math.log(0.3), math.log(3.0)))
    sample_base = jax.random.normal(subkeys[0], full_shape, jnp.float32)
    cell_scale = (row_rise * row_scale)[None, :, None, None] * col_scale[None, None, :, None]
    return (sample_base * cell_scale).astype(jnp.bfloat16)


def bell_draw(rng, dims, scale, reach, kind=jnp.bfloat16):
    result = jax.random.normal(rng, dims, jnp.float32) * scale
    return jnp.minimum(jnp.maximum(result, -reach), reach).astype(kind)


def setup_inputs(seed: int = 0, part: int = 0) -> dict:
    arg_keys = jax.random.split(jax.random.key(seed), 9)
    part_keys = jax.random.split(jax.random.fold_in(arg_keys[8], part), 9)
    return {
        "noisy_video": draw_noisy_video(jax.random.fold_in(jax.random.fold_in(arg_keys[8], part), 71), part),
        "timestep": jax.random.randint(part_keys[1], (1,), 100, 900).astype(jnp.int32),
        "embed_weight": bell_draw(arg_keys[2], (EMBED, 2 * CHANNELS), EMBED ** -0.5, 0.25),
        "norm_gain": jnp.clip(1.0 + 0.18 * jax.random.normal(arg_keys[3], (2, CHANNELS), jnp.float32), 0.1, 1.9),
        "norm_bias": bell_draw(arg_keys[4], (2, CHANNELS), 0.4, 2.4, jnp.float32),
        "conv_first": bell_draw(arg_keys[5], (3, 3, CHANNELS, CHANNELS), (9 * CHANNELS) ** -0.5, 0.1875),
        "temporal_weight": bell_draw(arg_keys[6], (3, CHANNELS, CHANNELS), (3 * CHANNELS) ** -0.5, 0.3125),
        "conv_second": bell_draw(arg_keys[7], (3, 3, CHANNELS, CHANNELS), (9 * CHANNELS) ** -0.5, 0.1875),
    }


def signal_noise(step_value):
    frac = (step_value.astype(jnp.float32) / TSTEPS + 0.008) / 1.008
    level = jnp.cos(frac * (math.pi / 2)) ** 2
    return (jnp.sqrt(level), jnp.sqrt(1.0 - level))

def embed_time(step_value, embed_weight):
    half = embed_weight.shape[0] // 2
    freqs = jnp.exp(-math.log(10000.0) * jnp.arange(half, dtype=jnp.float32) / half)
    angles = step_value.astype(jnp.float32) * freqs
    feats = jnp.concatenate([jnp.sin(angles), jnp.cos(angles)]).astype(jnp.bfloat16)
    film = jnp.dot(feats[None, :], embed_weight, preferred_element_type=jnp.float32)[0]
    channels = embed_weight.shape[1] // 2
    return (film[:channels], film[channels:])

def group_norm(values, gain, bias):
    frames, height, width, channels = values.shape
    grouped = values.reshape(frames, height, width, GROUPS, channels // GROUPS)
    first = lax.optimization_barrier(jnp.sum(grouped, axis=(1, 2, 4)))
    second = lax.optimization_barrier(jnp.sum(grouped * grouped, axis=(1, 2, 4)))
    count = height * width * (channels // GROUPS)
    mean = first / count
    inverse = lax.rsqrt(second / count - mean * mean + 1e-05)
    mean_ch = jnp.repeat(mean, channels // GROUPS, axis=1)[:, None, None, :]
    inv_ch = jnp.repeat(inverse, channels // GROUPS, axis=1)[:, None, None, :]
    return (values - mean_ch) * inv_ch * gain + bias

def spatial_conv(values, kernel):
    frames, height, width, channels = values.shape
    padded = jnp.pad(values, ((0, 0), (1, 1), (1, 1), (0, 0)))
    total = jnp.zeros((frames * height * width, kernel.shape[3]), jnp.float32)
    for offset_row in range(3):
        for offset_col in range(3):
            window = padded[:, offset_row:offset_row + height, offset_col:offset_col + width, :]
            total = total + jnp.dot(window.reshape(-1, channels), kernel[offset_row, offset_col], preferred_element_type=jnp.float32)
    return total.reshape(frames, height, width, kernel.shape[3])

def reference(noisy_video, timestep, embed_weight, norm_gain, norm_bias, conv_first, temporal_weight, conv_second):
    step_now = timestep[0]
    scale, shift = embed_time(step_now, embed_weight)
    signal_now, noise_now = signal_noise(step_now)
    signal_prev, noise_prev = signal_noise(step_now - STRIDE)
    video = noisy_video.astype(jnp.float32)
    activated = jax.nn.silu(group_norm(video, norm_gain[0], norm_bias[0])).astype(jnp.bfloat16)
    first = (spatial_conv(activated, conv_first) * (1.0 + scale) + shift).astype(jnp.bfloat16)
    mixed = jax.nn.silu(group_norm(first.astype(jnp.float32), norm_gain[1], norm_bias[1])).astype(jnp.bfloat16)
    frames, height, width, channels = mixed.shape
    framed = jnp.pad(mixed, ((1, 1), (0, 0), (0, 0), (0, 0)))
    total = jnp.zeros((frames * height * width, channels), jnp.float32)
    for offset in range(3):
        total = total + jnp.dot(framed[offset:offset + frames].reshape(-1, channels), temporal_weight[offset], preferred_element_type=jnp.float32)
    temporal = total.reshape(frames, height, width, channels).astype(jnp.bfloat16)
    predicted = (video + spatial_conv(temporal, conv_second)) * (1.0 / math.sqrt(2.0))
    estimate = (video - noise_now * predicted) / signal_now
    return ((signal_prev * estimate + noise_prev * predicted).astype(jnp.bfloat16), predicted)
```

```python
import functools
import math

import jax
import jax.numpy as jnp
import numpy as np
from jax import lax
from jax.experimental import pallas as pl
from jax.experimental.pallas import tpu as pltpu
from jax.sharding import PartitionSpec as P

GROUPS = 32
TSTEPS = 1000
STRIDE = 8
F32 = jnp.float32
BF16 = jnp.bfloat16
MESH = pl.DeviceIdType.MESH


def signal_noise(step_value):
    frac = (step_value / TSTEPS + 0.008) / 1.008
    level = jnp.cos(frac * (math.pi / 2)) ** 2
    return (jnp.sqrt(level), jnp.sqrt(1.0 - level))


def half_factors(stat, count, gain, bias):
    channels = stat.shape[1]
    size = channels // GROUPS
    row = lax.broadcasted_iota(jnp.int32, (channels, channels), 0) // size
    col = lax.broadcasted_iota(jnp.int32, (channels, channels), 1) // size
    same = jnp.where(row == col, 1.0, 0.0).astype(F32)
    sums = jnp.dot(stat, same, precision=lax.Precision.HIGHEST, preferred_element_type=F32)
    mean = sums[0:1] / count
    inverse = lax.rsqrt(sums[1:2] / count - mean * mean + 1e-05)
    a = inverse * gain
    return 0.5 * a, 0.5 * (bias - mean * a)


def half_silu(h):
    return h + h * jnp.tanh(h)


def put_taps(dst_ref, row, value):
    width, channels = value.shape
    pos = lax.broadcasted_iota(jnp.int32, value.shape, 0)
    left = jnp.where(pos == 0, 0.0, pltpu.roll(value, 1, 0))
    right = jnp.where(pos == width - 1, 0.0, pltpu.roll(value, width - 1, 0))
    dst_ref[row, :, 0:channels] = left.astype(BF16)
    dst_ref[row, :, channels : 2 * channels] = value.astype(BF16)
    dst_ref[row, :, 2 * channels : 3 * channels] = right.astype(BF16)


def put_weights(wide_ref, w_ref):
    channels = w_ref.shape[-1]
    for i in range(4):
        for o in range(2):
            for b in range(3):
                k = (i * 3 + b) * channels
                tap = i - o
                block = (
                    w_ref[tap, b]
                    if 0 <= tap <= 2
                    else jnp.zeros((channels, channels), BF16)
                )
                wide_ref[k : k + channels, o * channels : (o + 1) * channels] = block


def pair_dot(taps_ref, base, cols, wide_ref):
    lhs = jnp.concatenate([taps_ref[base + i, cols, :] for i in range(4)], axis=1)
    return jnp.dot(lhs, wide_ref[...], preferred_element_type=F32)


def fold8(x):
    return jnp.sum(x.reshape(x.shape[0] // 8, 8, x.shape[1]), axis=0)


def front(
    n,
    t_ref,
    video_ref,
    freqs_ref,
    embed_ref,
    gain_ref,
    bias_ref,
    w_ref,
    firsts_ref,
    stat_ref,
    halo,
    act,
    wide,
    first,
    s1_send,
    s1_recv,
    s2_send,
    s2_recv,
    sums,
    halo_ss,
    halo_rs,
    s1_ss,
    s1_rs,
    s2_ss,
    s2_rs,
    core_ss,
    core_rs,
    edge_ss,
    edge_rs,
    own_sem,
):
    height, width, channels = video_ref.shape
    pairs = height // 2
    f = lax.axis_index("frames")
    r = lax.axis_index("rows")
    me = f * n + r
    barrier = pltpu.get_barrier_semaphore()

    def peer(d):
        q = lax.rem(me + d, 2 * n)
        return q, {"frames": q // n, "rows": lax.rem(q, n)}

    @pl.loop(1, 2 * n)
    def _(d):
        _, device = peer(d)
        pl.semaphore_signal(barrier, 1, device_id=device, device_id_type=MESH)

    sums[...] = jnp.zeros_like(sums)

    @pl.loop(0, height)
    def _(h):
        x = video_ref[h].astype(F32)
        sums[0] += fold8(x)
        sums[1] += fold8(x * x)

    s1_send[...] = jnp.zeros_like(s1_send)
    s1_send[0:1] = jnp.sum(sums[0], axis=0, keepdims=True)
    s1_send[1:2] = jnp.sum(sums[1], axis=0, keepdims=True)
    s1_recv[r] = s1_send[...]
    pl.semaphore_wait(barrier, 2 * n - 1)

    def s1_copy(src_row, dst_row):
        return pltpu.make_async_remote_copy(
            s1_send,
            s1_recv.at[src_row],
            s1_ss.at[dst_row],
            s1_rs.at[src_row],
            device_id={"frames": f, "rows": dst_row},
            device_id_type=MESH,
        )

    @pl.loop(1, n)
    def _(d):
        s1_copy(r, lax.rem(r + d, n)).start()

    def halo_copy(side, target):
        return pltpu.make_async_remote_copy(
            video_ref.at[height - 1 if side == 0 else 0],
            halo.at[side],
            halo_ss.at[side],
            halo_rs.at[side],
            device_id={"frames": f, "rows": target},
            device_id_type=MESH,
        )

    has_low = r > 0
    has_high = r < n - 1

    @pl.when(has_high)
    def _():
        halo_copy(0, r + 1).start()

    @pl.when(has_low)
    def _():
        halo_copy(1, r - 1).start()

    put_weights(wide, w_ref)
    angles = t_ref[0].astype(F32) * jnp.broadcast_to(freqs_ref[...], (16, freqs_ref.shape[1]))
    feats = jnp.concatenate([jnp.sin(angles), jnp.cos(angles)], axis=1).astype(BF16)
    film = jnp.dot(feats, embed_ref[...], preferred_element_type=F32)[0:1]
    scale = 1.0 + film[:, :channels]
    shift = film[:, channels:]

    @pl.loop(1, n)
    def _(d):
        q = lax.rem(r + d, n)
        s1_copy(q, q).wait_recv()

    count = float(height * n * width * (channels // GROUPS))
    a, b = half_factors(jnp.sum(s1_recv[...], axis=0), count, gain_ref[0:1], bias_ref[0:1])

    def activate(x, row):
        h = x.astype(F32) * a + b
        put_taps(act, row, half_silu(h).astype(BF16).astype(F32))

    @pl.loop(0, height)
    def _(h):
        activate(video_ref[h], h + 1)

    zeros = jnp.zeros((width, 3 * channels), BF16)

    @pl.when(has_low)
    def _():
        halo_copy(0, r - 1).wait_recv()
        activate(halo[0], 0)

    @pl.when(r == 0)
    def _():
        act[0] = zeros

    @pl.when(has_high)
    def _():
        halo_copy(1, r + 1).wait_recv()
        activate(halo[1], height + 1)

    @pl.when(r == n - 1)
    def _():
        act[height + 1] = zeros

    def core_copy(p):
        return pltpu.make_async_remote_copy(
            first.at[pl.ds(2 * p, 2)],
            firsts_ref.at[1, pl.ds(1 + 2 * p, 2)],
            core_ss.at[p],
            core_rs.at[p],
            device_id={"frames": 1 - f, "rows": r},
            device_id_type=MESH,
        )

    def own_copy(p):
        return pltpu.make_async_copy(
            first.at[pl.ds(2 * p, 2)], firsts_ref.at[0, pl.ds(1 + 2 * p, 2)], own_sem.at[p]
        )

    def edge_copy(side, other, target):
        return pltpu.make_async_remote_copy(
            first.at[height - 1 if side == 0 else 0],
            firsts_ref.at[other, 0 if side == 0 else height + 1],
            edge_ss.at[side, other],
            edge_rs.at[side, other],
            device_id={"frames": 1 - f if other else f, "rows": target},
            device_id_type=MESH,
        )

    sums[...] = jnp.zeros_like(sums)
    step = width // 2
    order = [0] + ([pairs - 1] if pairs > 1 else []) + list(range(1, pairs - 1))
    for p in order:

        @pl.loop(0, width // step)
        def _(c):
            cols = pl.ds(pl.multiple_of(c * step, step), step)
            acc = pair_dot(act, 2 * p, cols, wide)
            for o in range(2):
                out = (acc[:, o * channels : (o + 1) * channels] * scale + shift).astype(BF16)
                first[2 * p + o, cols, :] = out
                value = out.astype(F32)
                sums[0] += fold8(value)
                sums[1] += fold8(value * value)

        core_copy(p).start()
        own_copy(p).start()
        if p == 0:

            @pl.when(has_low)
            def _():
                edge_copy(1, 0, r - 1).start()
                edge_copy(1, 1, r - 1).start()

        if p == pairs - 1:

            @pl.when(has_high)
            def _():
                edge_copy(0, 0, r + 1).start()
                edge_copy(0, 1, r + 1).start()

    s2_send[...] = jnp.zeros_like(s2_send)
    s2_send[0:1] = jnp.sum(sums[0], axis=0, keepdims=True)
    s2_send[1:2] = jnp.sum(sums[1], axis=0, keepdims=True)
    s2_recv[me] = s2_send[...]

    def s2_copy(source, q, device):
        return pltpu.make_async_remote_copy(
            s2_send,
            s2_recv.at[source],
            s2_ss.at[q],
            s2_rs.at[source],
            device_id=device,
            device_id_type=MESH,
        )

    @pl.loop(1, 2 * n)
    def _(d):
        q, device = peer(d)
        s2_copy(me, q, device).start()

    @pl.loop(1, 2 * n)
    def _(d):
        q, device = peer(d)
        s2_copy(q, q, device).wait_recv()

    stat_ref[0] = jnp.sum(s2_recv[pl.ds(f * n, n)], axis=0)
    stat_ref[1] = jnp.sum(s2_recv[pl.ds((1 - f) * n, n)], axis=0)

    for p in range(pairs):
        core_copy(p).wait()
        own_copy(p).wait()

    @pl.when(has_low)
    def _():
        halo_copy(1, r - 1).wait_send()
        for other in range(2):
            edge_copy(1, other, r - 1).wait_send()
            edge_copy(0, other, r - 1).wait_recv()

    @pl.when(has_high)
    def _():
        halo_copy(0, r + 1).wait_send()
        for other in range(2):
            edge_copy(0, other, r + 1).wait_send()
            edge_copy(1, other, r + 1).wait_recv()

    @pl.loop(1, n)
    def _(d):
        s1_copy(r, lax.rem(r + d, n)).wait_send()

    @pl.loop(1, 2 * n)
    def _(d):
        q, device = peer(d)
        s2_copy(me, q, device).wait_send()


def back(
    n,
    t_ref,
    firsts_ref,
    stat_ref,
    video_ref,
    gain_ref,
    bias_ref,
    tw_ref,
    w_ref,
    next_ref,
    pred_ref,
    taps,
    wide,
    wtime,
    factors,
    *,
    height,
):
    width, channels = firsts_ref.shape[2:]
    s = pl.program_id(0)
    f = lax.axis_index("frames")
    r = lax.axis_index("rows")

    @pl.when(s == 0)
    def _():
        put_weights(wide, w_ref)
        wtime[0:channels] = tw_ref[1]
        wtime[channels : 2 * channels] = tw_ref[2 - 2 * f]
        count = float(height * n * width * (channels // GROUPS))
        for i in range(2):
            a, b = half_factors(stat_ref[i], count, gain_ref[1:2], bias_ref[1:2])
            factors[2 * i : 2 * i + 1] = a
            factors[2 * i + 1 : 2 * i + 2] = b
        step_now = jnp.full((8, channels), t_ref[0].astype(F32))
        signal_now, noise_now = signal_noise(step_now)
        signal_prev, noise_prev = signal_noise(step_now - STRIDE)
        ratio = signal_prev / signal_now
        factors[4:5] = ratio[0:1]
        factors[5:6] = (noise_prev - ratio * noise_now)[0:1]

    for j in range(2):
        row = 2 * s + j
        mixed = []
        for i in range(2):
            h = firsts_ref[i, j].astype(F32) * factors[2 * i : 2 * i + 1] + factors[
                2 * i + 1 : 2 * i + 2
            ]
            mixed.append(half_silu(h).astype(BF16))
        value = jnp.dot(
            jnp.concatenate(mixed, axis=1), wtime[...], preferred_element_type=F32
        )
        where = r * height + row - 1
        inside = jnp.logical_and(where >= 0, where < n * height)
        value = jnp.where(inside, value, 0.0)
        put_taps(taps, row, value.astype(BF16).astype(F32))

    @pl.when(s > 0)
    def _():
        step = width // 2

        @pl.loop(0, width // step)
        def _(c):
            cols = pl.ds(pl.multiple_of(c * step, step), step)
            acc = pair_dot(taps, 2 * (s - 1), cols, wide)
            for o in range(2):
                video = video_ref[o, cols, :].astype(F32)
                predicted = (video + acc[:, o * channels : (o + 1) * channels]) * (
                    1.0 / math.sqrt(2.0)
                )
                pred_ref[o, cols, :] = predicted
                next_ref[o, cols, :] = (
                    video * factors[4:5] + predicted * factors[5:6]
                ).astype(BF16)


def body(
    n,
    noisy_video,
    timestep,
    embed_weight,
    norm_gain,
    norm_bias,
    conv_first,
    temporal_weight,
    conv_second,
):
    _, height, width, channels = noisy_video.shape
    video = noisy_video[0]
    half = embed_weight.shape[0] // 2
    freqs = np.exp(
        np.float32(-math.log(10000.0)) * np.arange(half, dtype=np.float32) / np.float32(half)
    )[None, :]
    vmem = pl.BlockSpec(memory_space=pltpu.VMEM)
    smem = pl.BlockSpec(memory_space=pltpu.SMEM)
    dma = pltpu.SemaphoreType.DMA
    pairs = height // 2
    firsts, stat = pl.pallas_call(
        functools.partial(front, n),
        out_shape=(
            jax.ShapeDtypeStruct((2, height + 2, width, channels), BF16),
            jax.ShapeDtypeStruct((2, 8, channels), F32),
        ),
        in_specs=[smem] + [vmem] * 6,
        out_specs=(pl.BlockSpec(memory_space=pl.ANY), vmem),
        scratch_shapes=[
            pltpu.VMEM((2, width, channels), BF16),
            pltpu.VMEM((height + 2, width, 3 * channels), BF16),
            pltpu.VMEM((12 * channels, 2 * channels), BF16),
            pltpu.VMEM((height, width, channels), BF16),
            pltpu.VMEM((8, channels), F32),
            pltpu.VMEM((n, 8, channels), F32),
            pltpu.VMEM((8, channels), F32),
            pltpu.VMEM((2 * n, 8, channels), F32),
            pltpu.VMEM((2, 8, channels), F32),
            dma((2,)),
            dma((2,)),
            dma((n,)),
            dma((n,)),
            dma((2 * n,)),
            dma((2 * n,)),
            dma((pairs,)),
            dma((pairs,)),
            dma((2, 2)),
            dma((2, 2)),
            dma((pairs,)),
        ],
        compiler_params=pltpu.CompilerParams(
            collective_id=0, has_side_effects=True, vmem_limit_bytes=48 * 1024 * 1024
        ),
        name="front",
    )(timestep, video, jnp.asarray(freqs), embed_weight, norm_gain, norm_bias, conv_first)

    def whole(*shape):
        return pl.BlockSpec(shape, lambda s: (0,) * len(shape))

    def pair_block():
        return pl.BlockSpec((2, width, channels), lambda s: (jnp.maximum(s - 1, 0), 0, 0))

    next_video, predicted = pl.pallas_call(
        functools.partial(back, n, height=height),
        grid=(pairs + 1,),
        out_shape=(
            jax.ShapeDtypeStruct((height, width, channels), BF16),
            jax.ShapeDtypeStruct((height, width, channels), F32),
        ),
        in_specs=[
            smem,
            pl.BlockSpec((2, 2, width, channels), lambda s: (0, s, 0, 0)),
            whole(2, 8, channels),
            pair_block(),
            whole(*norm_gain.shape),
            whole(*norm_bias.shape),
            whole(*temporal_weight.shape),
            whole(*conv_second.shape),
        ],
        out_specs=(pair_block(), pair_block()),
        scratch_shapes=[
            pltpu.VMEM((height + 2, width, 3 * channels), BF16),
            pltpu.VMEM((12 * channels, 2 * channels), BF16),
            pltpu.VMEM((2 * channels, channels), BF16),
            pltpu.VMEM((8, channels), F32),
        ],
        compiler_params=pltpu.CompilerParams(vmem_limit_bytes=48 * 1024 * 1024),
        name="back",
    )(timestep, firsts, stat, video, norm_gain, norm_bias, temporal_weight, conv_second)
    return next_video[None], predicted[None]


def solution(mesh):
    bands = P(("clips", "frames"), "rows", None, None)
    in_specs = (bands, P("clips"), P(), P(), P(), P(), P(), P())
    return jax.shard_map(
        functools.partial(body, mesh.shape["rows"]),
        mesh=mesh,
        in_specs=in_specs,
        out_specs=(bands, bands),
        check_vma=False,
    )
```

```python
import functools
import math

import jax
import jax.numpy as jnp
import numpy as np
from jax import lax
from jax.experimental import pallas as pl
from jax.experimental.pallas import tpu as pltpu
from jax.sharding import PartitionSpec as P

GROUPS = 32
TSTEPS = 1000
STRIDE = 8
F32 = jnp.float32
BF16 = jnp.bfloat16
MESH = pl.DeviceIdType.MESH


def signal_noise(step_value):
    frac = (step_value / TSTEPS + 0.008) / 1.008
    level = jnp.cos(frac * (math.pi / 2)) ** 2
    return (jnp.sqrt(level), jnp.sqrt(1.0 - level))


def half_factors(stat, count, gain, bias):
    channels = stat.shape[1]
    size = channels // GROUPS
    row = lax.broadcasted_iota(jnp.int32, (channels, channels), 0) // size
    col = lax.broadcasted_iota(jnp.int32, (channels, channels), 1) // size
    same = jnp.where(row == col, 1.0, 0.0).astype(F32)
    sums = jnp.dot(stat, same, precision=lax.Precision.HIGHEST, preferred_element_type=F32)
    mean = sums[0:1] / count
    inverse = lax.rsqrt(sums[1:2] / count - mean * mean + 1e-05)
    a = inverse * gain
    return 0.5 * a, 0.5 * (bias - mean * a)


def half_silu(h):
    return h + h * jnp.tanh(h)


def put_taps(dst_ref, row, value):
    width, channels = value.shape
    pos = lax.broadcasted_iota(jnp.int32, value.shape, 0)
    left = jnp.where(pos == 0, 0.0, pltpu.roll(value, 1, 0))
    right = jnp.where(pos == width - 1, 0.0, pltpu.roll(value, width - 1, 0))
    dst_ref[row, :, 0:channels] = left.astype(BF16)
    dst_ref[row, :, channels : 2 * channels] = value.astype(BF16)
    dst_ref[row, :, 2 * channels : 3 * channels] = right.astype(BF16)


def put_weights(wide_ref, w_ref):
    channels = w_ref.shape[-1]
    for i in range(4):
        for o in range(2):
            for b in range(3):
                k = (i * 3 + b) * channels
                tap = i - o
                block = (
                    w_ref[tap, b]
                    if 0 <= tap <= 2
                    else jnp.zeros((channels, channels), BF16)
                )
                wide_ref[k : k + channels, o * channels : (o + 1) * channels] = block


def pair_dot(taps_ref, base, cols, wide_ref):
    lhs = jnp.concatenate([taps_ref[base + i, cols, :] for i in range(4)], axis=1)
    return jnp.dot(lhs, wide_ref[...], preferred_element_type=F32)


def fold8(x):
    return jnp.sum(x.reshape(x.shape[0] // 8, 8, x.shape[1]), axis=0)


def front(
    n,
    t_hbm,
    video_hbm,
    freqs_hbm,
    embed_hbm,
    gain_hbm,
    bias_hbm,
    w_hbm,
    tw_hbm,
    w2_hbm,
    firsts_ref,
    factors,
    wide2,
    wtime,
    t_ref,
    video_ref,
    freqs_ref,
    embed_ref,
    gain_ref,
    bias_ref,
    w_ref,
    tw_ref,
    w2_ref,
    load_sem,
    halo,
    act,
    wide,
    first,
    s1_send,
    s1_recv,
    s2_send,
    s2_recv,
    sums,
    halo_ss,
    halo_rs,
    s1_ss,
    s1_rs,
    s2_ss,
    s2_rs,
    core_ss,
    core_rs,
    edge_ss,
    edge_rs,
    relay_ss,
    relay_rs,
    own_sem,
):
    height, width, channels = video_ref.shape
    pairs = height // 2
    f = lax.axis_index("frames")
    r = lax.axis_index("rows")
    me = f * n + r
    barrier = pltpu.get_barrier_semaphore()
    loads = [
        pltpu.make_async_copy(src, dst, load_sem.at[i])
        for i, (src, dst) in enumerate(
            (
                (video_hbm, video_ref),
                (t_hbm, t_ref),
                (freqs_hbm, freqs_ref),
                (embed_hbm, embed_ref),
                (gain_hbm, gain_ref),
                (bias_hbm, bias_ref),
                (w_hbm, w_ref),
                (tw_hbm, tw_ref),
                (w2_hbm, w2_ref),
            )
        )
    ]
    for load in loads:
        load.start()

    def peer(d):
        q = lax.rem(me + d, 2 * n)
        return q, {"frames": q // n, "rows": lax.rem(q, n)}

    @pl.loop(1, 2 * n)
    def _(d):
        _, device = peer(d)
        pl.semaphore_signal(barrier, 1, device_id=device, device_id_type=MESH)

    pl.semaphore_wait(barrier, 2 * n - 1)

    def halo_copy(side, target):
        return pltpu.make_async_remote_copy(
            video_hbm.at[height - 1 if side == 0 else 0],
            halo.at[side],
            halo_ss.at[side],
            halo_rs.at[side],
            device_id={"frames": f, "rows": target},
            device_id_type=MESH,
        )

    has_low = r > 0
    has_high = r < n - 1

    @pl.when(has_high)
    def _():
        halo_copy(0, r + 1).start()

    @pl.when(has_low)
    def _():
        halo_copy(1, r - 1).start()

    loads[0].wait()
    sums[...] = jnp.zeros_like(sums)

    @pl.loop(0, height)
    def _(h):
        x = video_ref[h].astype(F32)
        sums[0] += fold8(x)
        sums[1] += fold8(x * x)

    s1_send[...] = jnp.zeros_like(s1_send)
    s1_send[0:1] = jnp.sum(sums[0], axis=0, keepdims=True)
    s1_send[1:2] = jnp.sum(sums[1], axis=0, keepdims=True)
    s1_recv[r] = s1_send[...]

    def s1_copy(src_row, dst_row):
        return pltpu.make_async_remote_copy(
            s1_send,
            s1_recv.at[src_row],
            s1_ss.at[dst_row],
            s1_rs.at[src_row],
            device_id={"frames": f, "rows": dst_row},
            device_id_type=MESH,
        )

    @pl.loop(1, n)
    def _(d):
        s1_copy(r, lax.rem(r + d, n)).start()

    for load in loads[1:]:
        load.wait()
    put_weights(wide, w_ref)
    put_weights(wide2, w2_ref)
    wtime[0:channels] = tw_ref[1]
    wtime[channels : 2 * channels] = tw_ref[2 - 2 * f]
    step_now = jnp.full((8, channels), t_ref[0].astype(F32))
    signal_now, noise_now = signal_noise(step_now)
    signal_prev, noise_prev = signal_noise(step_now - STRIDE)
    ratio = signal_prev / signal_now
    factors[...] = jnp.zeros_like(factors)
    factors[4:5] = ratio[0:1]
    factors[5:6] = (noise_prev - ratio * noise_now)[0:1]
    angles = t_ref[0].astype(F32) * jnp.broadcast_to(freqs_ref[...], (16, freqs_ref.shape[1]))
    feats = jnp.concatenate([jnp.sin(angles), jnp.cos(angles)], axis=1).astype(BF16)
    film = jnp.dot(feats, embed_ref[...], preferred_element_type=F32)[0:1]
    scale = 1.0 + film[:, :channels]
    shift = film[:, channels:]

    @pl.loop(1, n)
    def _(d):
        q = lax.rem(r + d, n)
        s1_copy(q, q).wait_recv()

    count = float(height * n * width * (channels // GROUPS))
    a, b = half_factors(jnp.sum(s1_recv[...], axis=0), count, gain_ref[0:1], bias_ref[0:1])

    def activate(x, row):
        h = x.astype(F32) * a + b
        put_taps(act, row, half_silu(h).astype(BF16).astype(F32))

    @pl.loop(0, height)
    def _(h):
        activate(video_ref[h], h + 1)

    def core_copy(p):
        return pltpu.make_async_remote_copy(
            first.at[pl.ds(2 * p, 2)],
            firsts_ref.at[1, pl.ds(1 + 2 * p, 2)],
            core_ss.at[p],
            core_rs.at[p],
            device_id={"frames": 1 - f, "rows": r},
            device_id_type=MESH,
        )

    def own_copy(p):
        return pltpu.make_async_copy(
            first.at[pl.ds(2 * p, 2)], firsts_ref.at[0, pl.ds(1 + 2 * p, 2)], own_sem.at[p]
        )

    def edge_copy(side, target):
        return pltpu.make_async_remote_copy(
            first.at[height - 1 if side == 0 else 0],
            firsts_ref.at[0, 0 if side == 0 else height + 1],
            edge_ss.at[side],
            edge_rs.at[side],
            device_id={"frames": f, "rows": target},
            device_id_type=MESH,
        )

    def relay_copy(side):
        row = 0 if side == 0 else height + 1
        return pltpu.make_async_remote_copy(
            firsts_ref.at[0, row],
            firsts_ref.at[1, row],
            relay_ss.at[side],
            relay_rs.at[side],
            device_id={"frames": 1 - f, "rows": r},
            device_id_type=MESH,
        )

    sums[...] = jnp.zeros_like(sums)
    step = width // 2

    def convolve(p):
        @pl.loop(0, width // step)
        def _(c):
            cols = pl.ds(pl.multiple_of(c * step, step), step)
            acc = pair_dot(act, 2 * p, cols, wide)
            for o in range(2):
                out = (acc[:, o * channels : (o + 1) * channels] * scale + shift).astype(BF16)
                first[2 * p + o, cols, :] = out
                value = out.astype(F32)
                sums[0] += fold8(value)
                sums[1] += fold8(value * value)

        core_copy(p).start()
        own_copy(p).start()

    for p in range(1, pairs - 1):
        convolve(p)

    zeros = jnp.zeros((width, 3 * channels), BF16)

    @pl.when(has_low)
    def _():
        halo_copy(0, r - 1).wait_recv()
        activate(halo[0], 0)

    @pl.when(r == 0)
    def _():
        act[0] = zeros

    if pairs > 1:
        convolve(0)

        @pl.when(has_low)
        def _():
            edge_copy(1, r - 1).start()

    @pl.when(has_high)
    def _():
        halo_copy(1, r + 1).wait_recv()
        activate(halo[1], height + 1)

    @pl.when(r == n - 1)
    def _():
        act[height + 1] = zeros

    convolve(pairs - 1)

    @pl.when(has_high)
    def _():
        edge_copy(0, r + 1).start()

    if pairs == 1:

        @pl.when(has_low)
        def _():
            edge_copy(1, r - 1).start()

    s2_send[...] = jnp.zeros_like(s2_send)
    s2_send[0:1] = jnp.sum(sums[0], axis=0, keepdims=True)
    s2_send[1:2] = jnp.sum(sums[1], axis=0, keepdims=True)
    s2_recv[me] = s2_send[...]

    def s2_copy(source, q, device):
        return pltpu.make_async_remote_copy(
            s2_send,
            s2_recv.at[source],
            s2_ss.at[q],
            s2_rs.at[source],
            device_id=device,
            device_id_type=MESH,
        )

    @pl.loop(1, 2 * n)
    def _(d):
        q, device = peer(d)
        s2_copy(me, q, device).start()

    @pl.loop(1, 2 * n)
    def _(d):
        q, device = peer(d)
        s2_copy(q, q, device).wait_recv()

    for i in range(2):
        frame = f if i == 0 else 1 - f
        stat = jnp.sum(s2_recv[pl.ds(frame * n, n)], axis=0)
        a, b = half_factors(stat, count, gain_ref[1:2], bias_ref[1:2])
        factors[2 * i : 2 * i + 1] = a
        factors[2 * i + 1 : 2 * i + 2] = b

    @pl.when(has_low)
    def _():
        edge_copy(0, r - 1).wait_recv()
        relay_copy(0).start()

    @pl.when(has_high)
    def _():
        edge_copy(1, r + 1).wait_recv()
        relay_copy(1).start()

    for p in range(pairs):
        core_copy(p).wait()
        own_copy(p).wait()

    @pl.when(has_low)
    def _():
        halo_copy(1, r - 1).wait_send()
        edge_copy(1, r - 1).wait_send()
        relay_copy(0).wait()

    @pl.when(has_high)
    def _():
        halo_copy(0, r + 1).wait_send()
        edge_copy(0, r + 1).wait_send()
        relay_copy(1).wait()

    @pl.loop(1, n)
    def _(d):
        s1_copy(r, lax.rem(r + d, n)).wait_send()

    @pl.loop(1, 2 * n)
    def _(d):
        q, device = peer(d)
        s2_copy(me, q, device).wait_send()


def back(
    n, firsts_ref, factors, video_ref, wtime, wide, next_ref, pred_ref, taps, *, height
):
    width, channels = firsts_ref.shape[2:]
    s = pl.program_id(0)
    r = lax.axis_index("rows")

    for j in range(2):
        row = 2 * s + j
        mixed = []
        for i in range(2):
            h = firsts_ref[i, j].astype(F32) * factors[2 * i : 2 * i + 1] + factors[
                2 * i + 1 : 2 * i + 2
            ]
            mixed.append(half_silu(h).astype(BF16))
        value = jnp.dot(
            jnp.concatenate(mixed, axis=1), wtime[...], preferred_element_type=F32
        )
        where = r * height + row - 1
        inside = jnp.logical_and(where >= 0, where < n * height)
        value = jnp.where(inside, value, 0.0)
        put_taps(taps, row, value.astype(BF16).astype(F32))

    @pl.when(s > 0)
    def _():
        step = width // 2

        @pl.loop(0, width // step)
        def _(c):
            cols = pl.ds(pl.multiple_of(c * step, step), step)
            acc = pair_dot(taps, 2 * (s - 1), cols, wide)
            for o in range(2):
                video = video_ref[o, cols, :].astype(F32)
                predicted = (video + acc[:, o * channels : (o + 1) * channels]) * (
                    1.0 / math.sqrt(2.0)
                )
                pred_ref[o, cols, :] = predicted
                next_ref[o, cols, :] = (
                    video * factors[4:5] + predicted * factors[5:6]
                ).astype(BF16)


def body(
    n,
    noisy_video,
    timestep,
    embed_weight,
    norm_gain,
    norm_bias,
    conv_first,
    temporal_weight,
    conv_second,
):
    _, height, width, channels = noisy_video.shape
    video = noisy_video[0]
    half = embed_weight.shape[0] // 2
    freqs = np.exp(
        np.float32(-math.log(10000.0)) * np.arange(half, dtype=np.float32) / np.float32(half)
    )[None, :]
    vmem = pl.BlockSpec(memory_space=pltpu.VMEM)
    hbm = pl.BlockSpec(memory_space=pltpu.HBM)
    dma = pltpu.SemaphoreType.DMA
    pairs = height // 2
    args = (
        timestep,
        video,
        jnp.asarray(freqs),
        embed_weight,
        norm_gain,
        norm_bias,
        conv_first,
        temporal_weight,
        conv_second,
    )
    firsts, factors, wide2, wtime = pl.pallas_call(
        functools.partial(front, n),
        out_shape=(
            jax.ShapeDtypeStruct((2, height + 2, width, channels), BF16),
            jax.ShapeDtypeStruct((8, channels), F32),
            jax.ShapeDtypeStruct((12 * channels, 2 * channels), BF16),
            jax.ShapeDtypeStruct((2 * channels, channels), BF16),
        ),
        in_specs=[hbm] * len(args),
        out_specs=(hbm, vmem, vmem, vmem),
        scratch_shapes=[
            pltpu.SMEM(timestep.shape, timestep.dtype),
            *[pltpu.VMEM(x.shape, x.dtype) for x in args[1:]],
            dma((len(args),)),
            pltpu.VMEM((2, width, channels), BF16),
            pltpu.VMEM((height + 2, width, 3 * channels), BF16),
            pltpu.VMEM((12 * channels, 2 * channels), BF16),
            pltpu.VMEM((height, width, channels), BF16),
            pltpu.VMEM((8, channels), F32),
            pltpu.VMEM((n, 8, channels), F32),
            pltpu.VMEM((8, channels), F32),
            pltpu.VMEM((2 * n, 8, channels), F32),
            pltpu.VMEM((2, 8, channels), F32),
            dma((2,)),
            dma((2,)),
            dma((n,)),
            dma((n,)),
            dma((2 * n,)),
            dma((2 * n,)),
            dma((pairs,)),
            dma((pairs,)),
            dma((2,)),
            dma((2,)),
            dma((2,)),
            dma((2,)),
            dma((pairs,)),
        ],
        compiler_params=pltpu.CompilerParams(
            collective_id=0, has_side_effects=True, vmem_limit_bytes=60 * 1024 * 1024
        ),
        name="front",
    )(*args)

    def pair_block():
        return pl.BlockSpec((2, width, channels), lambda s: (jnp.maximum(s - 1, 0), 0, 0))

    next_video, predicted = pl.pallas_call(
        functools.partial(back, n, height=height),
        grid=(pairs + 1,),
        out_shape=(
            jax.ShapeDtypeStruct((height, width, channels), BF16),
            jax.ShapeDtypeStruct((height, width, channels), F32),
        ),
        in_specs=[
            pl.BlockSpec((2, 2, width, channels), lambda s: (0, s, 0, 0)),
            vmem,
            pair_block(),
            vmem,
            vmem,
        ],
        out_specs=(pair_block(), pair_block()),
        scratch_shapes=[
            pltpu.VMEM((height + 2, width, 3 * channels), BF16),
        ],
        compiler_params=pltpu.CompilerParams(vmem_limit_bytes=60 * 1024 * 1024),
        name="back",
    )(firsts, factors, video, wtime, wide2)
    return next_video[None], predicted[None]


def solution(mesh):
    bands = P(("clips", "frames"), "rows", None, None)
    in_specs = (bands, P("clips"), P(), P(), P(), P(), P(), P())
    return jax.shard_map(
        functools.partial(body, mesh.shape["rows"]),
        mesh=mesh,
        in_specs=in_specs,
        out_specs=(bands, bands),
        check_vma=False,
    )
```

```python
import functools
import math

import jax
import jax.numpy as jnp
import numpy as np
from jax import lax
from jax.experimental import pallas as pl
from jax.experimental.pallas import tpu as pltpu
from jax.sharding import PartitionSpec as P

GROUPS = 32
TSTEPS = 1000
STRIDE = 8
F32 = jnp.float32
BF16 = jnp.bfloat16
MESH = pl.DeviceIdType.MESH


def signal_noise(step_value):
    frac = (step_value / TSTEPS + 0.008) / 1.008
    level = jnp.cos(frac * (math.pi / 2)) ** 2
    return (jnp.sqrt(level), jnp.sqrt(1.0 - level))


def half_factors(stat, count, gain, bias):
    channels = stat.shape[1]
    size = channels // GROUPS
    row = lax.broadcasted_iota(jnp.int32, (channels, channels), 0) // size
    col = lax.broadcasted_iota(jnp.int32, (channels, channels), 1) // size
    same = jnp.where(row == col, 1.0, 0.0).astype(F32)
    sums = jnp.dot(stat, same, precision=lax.Precision.HIGHEST, preferred_element_type=F32)
    mean = sums[0:1] / count
    inverse = lax.rsqrt(sums[1:2] / count - mean * mean + 1e-05)
    a = inverse * gain
    return 0.5 * a, 0.5 * (bias - mean * a)


def half_silu(h):
    return h + h * jnp.tanh(h)


def put_taps(dst_ref, row, value):
    width, channels = value.shape
    pos = lax.broadcasted_iota(jnp.int32, value.shape, 0)
    left = jnp.where(pos == 0, 0.0, pltpu.roll(value, 1, 0))
    right = jnp.where(pos == width - 1, 0.0, pltpu.roll(value, width - 1, 0))
    dst_ref[row, :, 0:channels] = left.astype(BF16)
    dst_ref[row, :, channels : 2 * channels] = value.astype(BF16)
    dst_ref[row, :, 2 * channels : 3 * channels] = right.astype(BF16)


def put_weights(wide_ref, w_ref):
    channels = w_ref.shape[-1]
    for i in range(4):
        for o in range(2):
            for b in range(3):
                k = (i * 3 + b) * channels
                tap = i - o
                block = (
                    w_ref[tap, b]
                    if 0 <= tap <= 2
                    else jnp.zeros((channels, channels), BF16)
                )
                wide_ref[k : k + channels, o * channels : (o + 1) * channels] = block


def pair_dot(taps_ref, base, cols, wide_ref):
    lhs = jnp.concatenate([taps_ref[base + i, cols, :] for i in range(4)], axis=1)
    return jnp.dot(lhs, wide_ref[...], preferred_element_type=F32)


def fold8(x):
    return jnp.sum(x.reshape(x.shape[0] // 8, 8, x.shape[1]), axis=0)


def front(
    n,
    t_hbm,
    video_hbm,
    freqs_hbm,
    embed_hbm,
    gain_hbm,
    bias_hbm,
    w_hbm,
    tw_hbm,
    w2_hbm,
    firsts_ref,
    factors,
    wide2,
    wtime,
    t_ref,
    video_ref,
    freqs_ref,
    embed_ref,
    gain_ref,
    bias_ref,
    w_ref,
    tw_ref,
    w2_ref,
    load_sem,
    halo,
    act,
    wide,
    first,
    s1_send,
    s1_recv,
    s2_send,
    s2_recv,
    sums,
    halo_ss,
    halo_rs,
    s1_ss,
    s1_rs,
    s2_ss,
    s2_rs,
    core_ss,
    core_rs,
    own_sem,
):
    height, width, channels = video_ref.shape
    pairs = height // 2
    f = lax.axis_index("frames")
    r = lax.axis_index("rows")
    me = f * n + r
    barrier = pltpu.get_barrier_semaphore()
    loads = [
        pltpu.make_async_copy(src, dst, load_sem.at[i])
        for i, (src, dst) in enumerate(
            (
                (video_hbm, video_ref),
                (t_hbm, t_ref),
                (freqs_hbm, freqs_ref),
                (embed_hbm, embed_ref),
                (gain_hbm, gain_ref),
                (bias_hbm, bias_ref),
                (w_hbm, w_ref),
                (tw_hbm, tw_ref),
                (w2_hbm, w2_ref),
            )
        )
    ]
    for load in loads:
        load.start()

    def peer(d):
        q = lax.rem(me + d, 2 * n)
        return q, {"frames": q // n, "rows": lax.rem(q, n)}

    @pl.loop(1, 2 * n)
    def _(d):
        _, device = peer(d)
        pl.semaphore_signal(barrier, 1, device_id=device, device_id_type=MESH)

    pl.semaphore_wait(barrier, 2 * n - 1)

    def halo_copy(side, target, k):
        return pltpu.make_async_remote_copy(
            video_hbm.at[height - 1 - k if side == 0 else k],
            halo.at[side, k],
            halo_ss.at[side, k],
            halo_rs.at[side, k],
            device_id={"frames": f, "rows": target},
            device_id_type=MESH,
        )

    has_low = r > 0
    has_high = r < n - 1

    @pl.when(has_high)
    def _():
        halo_copy(0, r + 1, 0).start()

    @pl.when(has_low)
    def _():
        halo_copy(1, r - 1, 0).start()

    loads[0].wait()
    sums[...] = jnp.zeros_like(sums)

    @pl.loop(0, height)
    def _(h):
        x = video_ref[h].astype(F32)
        sums[0] += fold8(x)
        sums[1] += fold8(x * x)

    s1_send[...] = jnp.zeros_like(s1_send)
    s1_send[0:1] = jnp.sum(sums[0], axis=0, keepdims=True)
    s1_send[1:2] = jnp.sum(sums[1], axis=0, keepdims=True)
    s1_recv[r] = s1_send[...]

    def s1_copy(src_row, dst_row):
        return pltpu.make_async_remote_copy(
            s1_send,
            s1_recv.at[src_row],
            s1_ss.at[dst_row],
            s1_rs.at[src_row],
            device_id={"frames": f, "rows": dst_row},
            device_id_type=MESH,
        )

    @pl.loop(1, n)
    def _(d):
        s1_copy(r, lax.rem(r + d, n)).start()

    for load in loads[1:]:
        load.wait()
    put_weights(wide, w_ref)
    put_weights(wide2, w2_ref)
    wtime[0:channels] = tw_ref[1]
    wtime[channels : 2 * channels] = tw_ref[2 - 2 * f]
    step_now = jnp.full((8, channels), t_ref[0].astype(F32))
    signal_now, noise_now = signal_noise(step_now)
    signal_prev, noise_prev = signal_noise(step_now - STRIDE)
    ratio = signal_prev / signal_now
    factors[...] = jnp.zeros_like(factors)
    factors[4:5] = ratio[0:1]
    factors[5:6] = (noise_prev - ratio * noise_now)[0:1]
    angles = t_ref[0].astype(F32) * jnp.broadcast_to(freqs_ref[...], (16, freqs_ref.shape[1]))
    feats = jnp.concatenate([jnp.sin(angles), jnp.cos(angles)], axis=1).astype(BF16)
    film = jnp.dot(feats, embed_ref[...], preferred_element_type=F32)[0:1]
    scale = 1.0 + film[:, :channels]
    shift = film[:, channels:]

    @pl.loop(1, n)
    def _(d):
        q = lax.rem(r + d, n)
        s1_copy(q, q).wait_recv()

    @pl.when(has_high)
    def _():
        halo_copy(0, r + 1, 1).start()

    @pl.when(has_low)
    def _():
        halo_copy(1, r - 1, 1).start()

    count = float(height * n * width * (channels // GROUPS))
    a, b = half_factors(jnp.sum(s1_recv[...], axis=0), count, gain_ref[0:1], bias_ref[0:1])

    def activate(x, row):
        h = x.astype(F32) * a + b
        put_taps(act, row, half_silu(h).astype(BF16).astype(F32))

    @pl.loop(0, height)
    def _(h):
        activate(video_ref[h], h + 2)

    def core_copy(p):
        return pltpu.make_async_remote_copy(
            first.at[pl.ds(1 + 2 * p, 2)],
            firsts_ref.at[1, pl.ds(1 + 2 * p, 2)],
            core_ss.at[p],
            core_rs.at[p],
            device_id={"frames": 1 - f, "rows": r},
            device_id_type=MESH,
        )

    def own_copy(p):
        return pltpu.make_async_copy(
            first.at[pl.ds(1 + 2 * p, 2)], firsts_ref.at[0, pl.ds(1 + 2 * p, 2)], own_sem.at[p]
        )

    def edge_copies(side):
        row = 0 if side == 0 else height + 1
        return (
            pltpu.make_async_remote_copy(
                first.at[row],
                firsts_ref.at[1, row],
                core_ss.at[pairs + side],
                core_rs.at[pairs + side],
                device_id={"frames": 1 - f, "rows": r},
                device_id_type=MESH,
            ),
            pltpu.make_async_copy(
                first.at[row], firsts_ref.at[0, row], own_sem.at[pairs + side]
            ),
        )

    sums[...] = jnp.zeros_like(sums)
    step = width // 2

    def convolve(p):
        @pl.loop(0, width // step)
        def _(c):
            cols = pl.ds(pl.multiple_of(c * step, step), step)
            acc = pair_dot(act, 2 * p + 1, cols, wide)
            for o in range(2):
                out = (acc[:, o * channels : (o + 1) * channels] * scale + shift).astype(BF16)
                first[1 + 2 * p + o, cols, :] = out
                value = out.astype(F32)
                sums[0] += fold8(value)
                sums[1] += fold8(value * value)

        core_copy(p).start()
        own_copy(p).start()

    for p in range(1, pairs - 1):
        convolve(p)

    zeros = jnp.zeros((width, 3 * channels), BF16)

    @pl.when(has_low)
    def _():
        halo_copy(0, r - 1, 0).wait_recv()
        activate(halo[0, 0], 1)

    @pl.when(r == 0)
    def _():
        act[1] = zeros

    if pairs > 1:
        convolve(0)

    @pl.when(has_high)
    def _():
        halo_copy(1, r + 1, 0).wait_recv()
        activate(halo[1, 0], height + 2)

    @pl.when(r == n - 1)
    def _():
        act[height + 2] = zeros

    convolve(pairs - 1)

    s2_send[...] = jnp.zeros_like(s2_send)
    s2_send[0:1] = jnp.sum(sums[0], axis=0, keepdims=True)
    s2_send[1:2] = jnp.sum(sums[1], axis=0, keepdims=True)
    s2_recv[me] = s2_send[...]

    def s2_copy(source, q, device):
        return pltpu.make_async_remote_copy(
            s2_send,
            s2_recv.at[source],
            s2_ss.at[q],
            s2_rs.at[source],
            device_id=device,
            device_id_type=MESH,
        )

    @pl.loop(1, 2 * n)
    def _(d):
        q, device = peer(d)
        s2_copy(me, q, device).start()

    def beyond(side):
        base = 0 if side == 0 else height
        row = 0 if side == 0 else height + 1

        @pl.loop(0, width // step)
        def _(c):
            cols = pl.ds(pl.multiple_of(c * step, step), step)
            acc = pair_dot(act, base, cols, wide)[:, side * channels : (side + 1) * channels]
            first[row, cols, :] = (acc * scale + shift).astype(BF16)

        for copy in edge_copies(side):
            copy.start()

    @pl.when(has_low)
    def _():
        halo_copy(0, r - 1, 1).wait_recv()
        activate(halo[0, 1], 0)
        beyond(0)

    @pl.when(has_high)
    def _():
        halo_copy(1, r + 1, 1).wait_recv()
        activate(halo[1, 1], height + 3)
        beyond(1)

    @pl.loop(1, 2 * n)
    def _(d):
        q, device = peer(d)
        s2_copy(q, q, device).wait_recv()

    for i in range(2):
        frame = f if i == 0 else 1 - f
        stat = jnp.sum(s2_recv[pl.ds(frame * n, n)], axis=0)
        a, b = half_factors(stat, count, gain_ref[1:2], bias_ref[1:2])
        factors[2 * i : 2 * i + 1] = a
        factors[2 * i + 1 : 2 * i + 2] = b

    for p in range(pairs):
        core_copy(p).wait()
        own_copy(p).wait()

    @pl.when(has_low)
    def _():
        for k in range(2):
            halo_copy(1, r - 1, k).wait_send()
        for copy in edge_copies(0):
            copy.wait()

    @pl.when(has_high)
    def _():
        for k in range(2):
            halo_copy(0, r + 1, k).wait_send()
        for copy in edge_copies(1):
            copy.wait()

    @pl.loop(1, n)
    def _(d):
        s1_copy(r, lax.rem(r + d, n)).wait_send()

    @pl.loop(1, 2 * n)
    def _(d):
        q, device = peer(d)
        s2_copy(me, q, device).wait_send()


def back(
    n, firsts_ref, factors, video_ref, wtime, wide, next_ref, pred_ref, taps, *, height
):
    width, channels = firsts_ref.shape[2:]
    s = pl.program_id(0)
    r = lax.axis_index("rows")

    for j in range(2):
        row = 2 * s + j
        mixed = []
        for i in range(2):
            h = firsts_ref[i, j].astype(F32) * factors[2 * i : 2 * i + 1] + factors[
                2 * i + 1 : 2 * i + 2
            ]
            mixed.append(half_silu(h).astype(BF16))
        value = jnp.dot(
            jnp.concatenate(mixed, axis=1), wtime[...], preferred_element_type=F32
        )
        where = r * height + row - 1
        inside = jnp.logical_and(where >= 0, where < n * height)
        value = jnp.where(inside, value, 0.0)
        put_taps(taps, row, value.astype(BF16).astype(F32))

    @pl.when(s > 0)
    def _():
        step = width // 2

        @pl.loop(0, width // step)
        def _(c):
            cols = pl.ds(pl.multiple_of(c * step, step), step)
            acc = pair_dot(taps, 2 * (s - 1), cols, wide)
            for o in range(2):
                video = video_ref[o, cols, :].astype(F32)
                predicted = (video + acc[:, o * channels : (o + 1) * channels]) * (
                    1.0 / math.sqrt(2.0)
                )
                pred_ref[o, cols, :] = predicted
                next_ref[o, cols, :] = (
                    video * factors[4:5] + predicted * factors[5:6]
                ).astype(BF16)


def body(
    n,
    noisy_video,
    timestep,
    embed_weight,
    norm_gain,
    norm_bias,
    conv_first,
    temporal_weight,
    conv_second,
):
    _, height, width, channels = noisy_video.shape
    video = noisy_video[0]
    half = embed_weight.shape[0] // 2
    freqs = np.exp(
        np.float32(-math.log(10000.0)) * np.arange(half, dtype=np.float32) / np.float32(half)
    )[None, :]
    vmem = pl.BlockSpec(memory_space=pltpu.VMEM)
    hbm = pl.BlockSpec(memory_space=pltpu.HBM)
    dma = pltpu.SemaphoreType.DMA
    pairs = height // 2
    args = (
        timestep,
        video,
        jnp.asarray(freqs),
        embed_weight,
        norm_gain,
        norm_bias,
        conv_first,
        temporal_weight,
        conv_second,
    )
    firsts, factors, wide2, wtime = pl.pallas_call(
        functools.partial(front, n),
        out_shape=(
            jax.ShapeDtypeStruct((2, height + 2, width, channels), BF16),
            jax.ShapeDtypeStruct((8, channels), F32),
            jax.ShapeDtypeStruct((12 * channels, 2 * channels), BF16),
            jax.ShapeDtypeStruct((2 * channels, channels), BF16),
        ),
        in_specs=[hbm] * len(args),
        out_specs=(hbm, vmem, vmem, vmem),
        scratch_shapes=[
            pltpu.SMEM(timestep.shape, timestep.dtype),
            *[pltpu.VMEM(x.shape, x.dtype) for x in args[1:]],
            dma((len(args),)),
            pltpu.VMEM((2, 2, width, channels), BF16),
            pltpu.VMEM((height + 4, width, 3 * channels), BF16),
            pltpu.VMEM((12 * channels, 2 * channels), BF16),
            pltpu.VMEM((height + 2, width, channels), BF16),
            pltpu.VMEM((8, channels), F32),
            pltpu.VMEM((n, 8, channels), F32),
            pltpu.VMEM((8, channels), F32),
            pltpu.VMEM((2 * n, 8, channels), F32),
            pltpu.VMEM((2, 8, channels), F32),
            dma((2, 2)),
            dma((2, 2)),
            dma((n,)),
            dma((n,)),
            dma((2 * n,)),
            dma((2 * n,)),
            dma((pairs + 2,)),
            dma((pairs + 2,)),
            dma((pairs + 2,)),
        ],
        compiler_params=pltpu.CompilerParams(
            collective_id=0, has_side_effects=True, vmem_limit_bytes=60 * 1024 * 1024
        ),
        name="front",
    )(*args)

    def pair_block():
        return pl.BlockSpec((2, width, channels), lambda s: (jnp.maximum(s - 1, 0), 0, 0))

    next_video, predicted = pl.pallas_call(
        functools.partial(back, n, height=height),
        grid=(pairs + 1,),
        out_shape=(
            jax.ShapeDtypeStruct((height, width, channels), BF16),
            jax.ShapeDtypeStruct((height, width, channels), F32),
        ),
        in_specs=[
            pl.BlockSpec((2, 2, width, channels), lambda s: (0, s, 0, 0)),
            vmem,
            pair_block(),
            vmem,
            vmem,
        ],
        out_specs=(pair_block(), pair_block()),
        scratch_shapes=[
            pltpu.VMEM((height + 2, width, 3 * channels), BF16),
        ],
        compiler_params=pltpu.CompilerParams(vmem_limit_bytes=60 * 1024 * 1024),
        name="back",
    )(firsts, factors, video, wtime, wide2)
    return next_video[None], predicted[None]


def solution(mesh):
    bands = P(("clips", "frames"), "rows", None, None)
    in_specs = (bands, P("clips"), P(), P(), P(), P(), P(), P())
    return jax.shard_map(
        functools.partial(body, mesh.shape["rows"]),
        mesh=mesh,
        in_specs=in_specs,
        out_specs=(bands, bands),
        check_vma=False,
    )
```

```python
import functools
import math

import jax
import jax.numpy as jnp
import numpy as np
from jax import lax
from jax.experimental import pallas as pl
from jax.experimental.pallas import tpu as pltpu
from jax.sharding import PartitionSpec as P

GROUPS = 32
TSTEPS = 1000
STRIDE = 8
F32 = jnp.float32
BF16 = jnp.bfloat16
MESH = pl.DeviceIdType.MESH


def signal_noise(step_value):
    frac = (step_value / TSTEPS + 0.008) / 1.008
    level = jnp.cos(frac * (math.pi / 2)) ** 2
    return (jnp.sqrt(level), jnp.sqrt(1.0 - level))


def half_factors(stat, count, gain, bias):
    channels = stat.shape[1]
    size = channels // GROUPS
    row = lax.broadcasted_iota(jnp.int32, (channels, channels), 0) // size
    col = lax.broadcasted_iota(jnp.int32, (channels, channels), 1) // size
    same = jnp.where(row == col, 1.0, 0.0).astype(F32)
    sums = jnp.dot(stat, same, precision=lax.Precision.HIGHEST, preferred_element_type=F32)
    mean = sums[0:1] / count
    inverse = lax.rsqrt(sums[1:2] / count - mean * mean + 1e-05)
    a = inverse * gain
    return 0.5 * a, 0.5 * (bias - mean * a)


def half_silu(h):
    return h + h * jnp.tanh(h)


def put_taps(dst_ref, row, value):
    width, channels = value.shape
    pos = lax.broadcasted_iota(jnp.int32, value.shape, 0)
    left = jnp.where(pos == 0, 0.0, pltpu.roll(value, 1, 0))
    right = jnp.where(pos == width - 1, 0.0, pltpu.roll(value, width - 1, 0))
    dst_ref[row, :, 0:channels] = left.astype(BF16)
    dst_ref[row, :, channels : 2 * channels] = value.astype(BF16)
    dst_ref[row, :, 2 * channels : 3 * channels] = right.astype(BF16)


def put_weights(wide_ref, w_ref):
    channels = w_ref.shape[-1]
    for i in range(4):
        for o in range(2):
            for b in range(3):
                k = (i * 3 + b) * channels
                tap = i - o
                block = (
                    w_ref[tap, b]
                    if 0 <= tap <= 2
                    else jnp.zeros((channels, channels), BF16)
                )
                wide_ref[k : k + channels, o * channels : (o + 1) * channels] = block


def pair_dot(taps_ref, base, cols, wide_ref):
    lhs = jnp.concatenate([taps_ref[base + i, cols, :] for i in range(4)], axis=1)
    return jnp.dot(lhs, wide_ref[...], preferred_element_type=F32)


def fold8(x):
    return jnp.sum(x.reshape(x.shape[0] // 8, 8, x.shape[1]), axis=0)


def front(
    n,
    t_hbm,
    video_hbm,
    freqs_hbm,
    embed_hbm,
    gain_hbm,
    bias_hbm,
    w_hbm,
    tw_hbm,
    w2_hbm,
    firsts_ref,
    factors,
    wide2,
    wtime,
    t_ref,
    video_ref,
    freqs_ref,
    embed_ref,
    gain_ref,
    bias_ref,
    w_ref,
    tw_ref,
    w2_ref,
    load_sem,
    halo,
    act,
    wide,
    first,
    s1_send,
    s1_recv,
    s2_send,
    s2_recv,
    sums,
    halo_ss,
    halo_rs,
    s1_ss,
    s1_rs,
    s2_ss,
    s2_rs,
    core_ss,
    core_rs,
    own_sem,
):
    height, width, channels = video_ref.shape
    pairs = height // 2
    f = lax.axis_index("frames")
    r = lax.axis_index("rows")
    me = f * n + r
    barrier = pltpu.get_barrier_semaphore()
    loads = [
        pltpu.make_async_copy(src, dst, load_sem.at[i])
        for i, (src, dst) in enumerate(
            (
                (video_hbm, video_ref),
                (t_hbm, t_ref),
                (freqs_hbm, freqs_ref),
                (embed_hbm, embed_ref),
                (gain_hbm, gain_ref),
                (bias_hbm, bias_ref),
                (w_hbm, w_ref),
                (tw_hbm, tw_ref),
                (w2_hbm, w2_ref),
            )
        )
    ]
    for load in loads:
        load.start()

    def peer(d):
        q = lax.rem(me + d, 2 * n)
        return q, {"frames": q // n, "rows": lax.rem(q, n)}

    @pl.loop(1, 2 * n)
    def _(d):
        _, device = peer(d)
        pl.semaphore_signal(barrier, 1, device_id=device, device_id_type=MESH)

    pl.semaphore_wait(barrier, 2 * n - 1)

    def halo_copy(side, target, k):
        return pltpu.make_async_remote_copy(
            video_hbm.at[height - 1 - k if side == 0 else k],
            halo.at[side, k],
            halo_ss.at[side, k],
            halo_rs.at[side, k],
            device_id={"frames": f, "rows": target},
            device_id_type=MESH,
        )

    has_low = r > 0
    has_high = r < n - 1

    @pl.when(has_high)
    def _():
        halo_copy(0, r + 1, 0).start()

    @pl.when(has_low)
    def _():
        halo_copy(1, r - 1, 0).start()

    loads[0].wait()
    sums[...] = jnp.zeros_like(sums)

    @pl.loop(0, height)
    def _(h):
        x = video_ref[h].astype(F32)
        sums[0] += fold8(x)
        sums[1] += fold8(x * x)

    s1_send[...] = jnp.zeros_like(s1_send)
    s1_send[0:1] = jnp.sum(sums[0], axis=0, keepdims=True)
    s1_send[1:2] = jnp.sum(sums[1], axis=0, keepdims=True)
    s1_recv[r] = s1_send[...]

    def s1_copy(src_row, dst_row):
        return pltpu.make_async_remote_copy(
            s1_send,
            s1_recv.at[src_row],
            s1_ss.at[dst_row],
            s1_rs.at[src_row],
            device_id={"frames": f, "rows": dst_row},
            device_id_type=MESH,
        )

    @pl.loop(1, n)
    def _(d):
        s1_copy(r, lax.rem(r + d, n)).start()

    for load in loads[1:]:
        load.wait()
    put_weights(wide, w_ref)
    put_weights(wide2, w2_ref)
    wtime[0:channels] = tw_ref[1]
    wtime[channels : 2 * channels] = tw_ref[2 - 2 * f]
    step_now = jnp.full((8, channels), t_ref[0].astype(F32))
    signal_now, noise_now = signal_noise(step_now)
    signal_prev, noise_prev = signal_noise(step_now - STRIDE)
    ratio = signal_prev / signal_now
    factors[...] = jnp.zeros_like(factors)
    factors[4:5] = ratio[0:1]
    factors[5:6] = (noise_prev - ratio * noise_now)[0:1]
    angles = t_ref[0].astype(F32) * jnp.broadcast_to(freqs_ref[...], (16, freqs_ref.shape[1]))
    feats = jnp.concatenate([jnp.sin(angles), jnp.cos(angles)], axis=1).astype(BF16)
    film = jnp.dot(feats, embed_ref[...], preferred_element_type=F32)[0:1]
    scale = 1.0 + film[:, :channels]
    shift = film[:, channels:]

    @pl.loop(1, n)
    def _(d):
        q = lax.rem(r + d, n)
        s1_copy(q, q).wait_recv()

    @pl.when(has_high)
    def _():
        halo_copy(0, r + 1, 1).start()

    @pl.when(has_low)
    def _():
        halo_copy(1, r - 1, 1).start()

    count = float(height * n * width * (channels // GROUPS))
    a, b = half_factors(jnp.sum(s1_recv[...], axis=0), count, gain_ref[0:1], bias_ref[0:1])

    def activate(x, row):
        h = x.astype(F32) * a + b
        put_taps(act, row, half_silu(h).astype(BF16).astype(F32))

    @pl.loop(0, height)
    def _(h):
        activate(video_ref[h], h + 2)

    def core_copy(p):
        return pltpu.make_async_remote_copy(
            first.at[pl.ds(1 + 2 * p, 2)],
            firsts_ref.at[1, pl.ds(1 + 2 * p, 2)],
            core_ss.at[p],
            core_rs.at[p],
            device_id={"frames": 1 - f, "rows": r},
            device_id_type=MESH,
        )

    def own_copy(p):
        return pltpu.make_async_copy(
            first.at[pl.ds(1 + 2 * p, 2)], firsts_ref.at[0, pl.ds(1 + 2 * p, 2)], own_sem.at[p]
        )

    def edge_copies(side):
        row = 0 if side == 0 else height + 1
        return (
            pltpu.make_async_remote_copy(
                first.at[row],
                firsts_ref.at[1, row],
                core_ss.at[pairs + side],
                core_rs.at[pairs + side],
                device_id={"frames": 1 - f, "rows": r},
                device_id_type=MESH,
            ),
            pltpu.make_async_copy(
                first.at[row], firsts_ref.at[0, row], own_sem.at[pairs + side]
            ),
        )

    sums[...] = jnp.zeros_like(sums)
    step = width

    def convolve(p):
        @pl.loop(0, width // step)
        def _(c):
            cols = pl.ds(pl.multiple_of(c * step, step), step)
            acc = pair_dot(act, 2 * p + 1, cols, wide)
            for o in range(2):
                out = (acc[:, o * channels : (o + 1) * channels] * scale + shift).astype(BF16)
                first[1 + 2 * p + o, cols, :] = out
                value = out.astype(F32)
                sums[0] += fold8(value)
                sums[1] += fold8(value * value)

        core_copy(p).start()
        own_copy(p).start()

    for p in range(1, pairs - 1):
        convolve(p)

    zeros = jnp.zeros((width, 3 * channels), BF16)

    @pl.when(has_low)
    def _():
        halo_copy(0, r - 1, 0).wait_recv()
        activate(halo[0, 0], 1)

    @pl.when(r == 0)
    def _():
        act[1] = zeros

    if pairs > 1:
        convolve(0)

    @pl.when(has_high)
    def _():
        halo_copy(1, r + 1, 0).wait_recv()
        activate(halo[1, 0], height + 2)

    @pl.when(r == n - 1)
    def _():
        act[height + 2] = zeros

    convolve(pairs - 1)

    s2_send[...] = jnp.zeros_like(s2_send)
    s2_send[0:1] = jnp.sum(sums[0], axis=0, keepdims=True)
    s2_send[1:2] = jnp.sum(sums[1], axis=0, keepdims=True)
    s2_recv[me] = s2_send[...]

    def s2_copy(source, q, device):
        return pltpu.make_async_remote_copy(
            s2_send,
            s2_recv.at[source],
            s2_ss.at[q],
            s2_rs.at[source],
            device_id=device,
            device_id_type=MESH,
        )

    @pl.loop(1, 2 * n)
    def _(d):
        q, device = peer(d)
        s2_copy(me, q, device).start()

    def beyond(side):
        base = 0 if side == 0 else height
        row = 0 if side == 0 else height + 1

        @pl.loop(0, width // step)
        def _(c):
            cols = pl.ds(pl.multiple_of(c * step, step), step)
            acc = pair_dot(act, base, cols, wide)[:, side * channels : (side + 1) * channels]
            first[row, cols, :] = (acc * scale + shift).astype(BF16)

        for copy in edge_copies(side):
            copy.start()

    @pl.when(has_low)
    def _():
        halo_copy(0, r - 1, 1).wait_recv()
        activate(halo[0, 1], 0)
        beyond(0)

    @pl.when(has_high)
    def _():
        halo_copy(1, r + 1, 1).wait_recv()
        activate(halo[1, 1], height + 3)
        beyond(1)

    @pl.loop(1, 2 * n)
    def _(d):
        q, device = peer(d)
        s2_copy(q, q, device).wait_recv()

    for i in range(2):
        frame = f if i == 0 else 1 - f
        stat = jnp.sum(s2_recv[pl.ds(frame * n, n)], axis=0)
        a, b = half_factors(stat, count, gain_ref[1:2], bias_ref[1:2])
        factors[2 * i : 2 * i + 1] = a
        factors[2 * i + 1 : 2 * i + 2] = b

    for p in range(pairs):
        core_copy(p).wait()
        own_copy(p).wait()

    @pl.when(has_low)
    def _():
        for k in range(2):
            halo_copy(1, r - 1, k).wait_send()
        for copy in edge_copies(0):
            copy.wait()

    @pl.when(has_high)
    def _():
        for k in range(2):
            halo_copy(0, r + 1, k).wait_send()
        for copy in edge_copies(1):
            copy.wait()

    @pl.loop(1, n)
    def _(d):
        s1_copy(r, lax.rem(r + d, n)).wait_send()

    @pl.loop(1, 2 * n)
    def _(d):
        q, device = peer(d)
        s2_copy(me, q, device).wait_send()


def back(
    n, firsts_ref, factors, video_ref, wtime, wide, next_ref, pred_ref, taps, *, height
):
    width, channels = firsts_ref.shape[2:]
    s = pl.program_id(0)
    r = lax.axis_index("rows")

    for j in range(2):
        row = 2 * s + j
        mixed = []
        for i in range(2):
            h = firsts_ref[i, j].astype(F32) * factors[2 * i : 2 * i + 1] + factors[
                2 * i + 1 : 2 * i + 2
            ]
            mixed.append(half_silu(h).astype(BF16))
        value = jnp.dot(
            jnp.concatenate(mixed, axis=1), wtime[...], preferred_element_type=F32
        )
        where = r * height + row - 1
        inside = jnp.logical_and(where >= 0, where < n * height)
        value = jnp.where(inside, value, 0.0)
        put_taps(taps, row, value.astype(BF16).astype(F32))

    @pl.when(s > 0)
    def _():
        step = width

        @pl.loop(0, width // step)
        def _(c):
            cols = pl.ds(pl.multiple_of(c * step, step), step)
            acc = pair_dot(taps, 2 * (s - 1), cols, wide)
            for o in range(2):
                video = video_ref[o, cols, :].astype(F32)
                predicted = (video + acc[:, o * channels : (o + 1) * channels]) * (
                    1.0 / math.sqrt(2.0)
                )
                pred_ref[o, cols, :] = predicted
                next_ref[o, cols, :] = (
                    video * factors[4:5] + predicted * factors[5:6]
                ).astype(BF16)


def body(
    n,
    noisy_video,
    timestep,
    embed_weight,
    norm_gain,
    norm_bias,
    conv_first,
    temporal_weight,
    conv_second,
):
    _, height, width, channels = noisy_video.shape
    video = noisy_video[0]
    half = embed_weight.shape[0] // 2
    freqs = np.exp(
        np.float32(-math.log(10000.0)) * np.arange(half, dtype=np.float32) / np.float32(half)
    )[None, :]
    vmem = pl.BlockSpec(memory_space=pltpu.VMEM)
    hbm = pl.BlockSpec(memory_space=pltpu.HBM)
    dma = pltpu.SemaphoreType.DMA
    pairs = height // 2
    args = (
        timestep,
        video,
        jnp.asarray(freqs),
        embed_weight,
        norm_gain,
        norm_bias,
        conv_first,
        temporal_weight,
        conv_second,
    )
    firsts, factors, wide2, wtime = pl.pallas_call(
        functools.partial(front, n),
        out_shape=(
            jax.ShapeDtypeStruct((2, height + 2, width, channels), BF16),
            jax.ShapeDtypeStruct((8, channels), F32),
            jax.ShapeDtypeStruct((12 * channels, 2 * channels), BF16),
            jax.ShapeDtypeStruct((2 * channels, channels), BF16),
        ),
        in_specs=[hbm] * len(args),
        out_specs=(hbm, vmem, vmem, vmem),
        scratch_shapes=[
            pltpu.SMEM(timestep.shape, timestep.dtype),
            *[pltpu.VMEM(x.shape, x.dtype) for x in args[1:]],
            dma((len(args),)),
            pltpu.VMEM((2, 2, width, channels), BF16),
            pltpu.VMEM((height + 4, width, 3 * channels), BF16),
            pltpu.VMEM((12 * channels, 2 * channels), BF16),
            pltpu.VMEM((height + 2, width, channels), BF16),
            pltpu.VMEM((8, channels), F32),
            pltpu.VMEM((n, 8, channels), F32),
            pltpu.VMEM((8, channels), F32),
            pltpu.VMEM((2 * n, 8, channels), F32),
            pltpu.VMEM((2, 8, channels), F32),
            dma((2, 2)),
            dma((2, 2)),
            dma((n,)),
            dma((n,)),
            dma((2 * n,)),
            dma((2 * n,)),
            dma((pairs + 2,)),
            dma((pairs + 2,)),
            dma((pairs + 2,)),
        ],
        compiler_params=pltpu.CompilerParams(
            collective_id=0, has_side_effects=True, vmem_limit_bytes=60 * 1024 * 1024
        ),
        name="front",
    )(*args)

    def pair_block():
        return pl.BlockSpec((2, width, channels), lambda s: (jnp.maximum(s - 1, 0), 0, 0))

    next_video, predicted = pl.pallas_call(
        functools.partial(back, n, height=height),
        grid=(pairs + 1,),
        out_shape=(
            jax.ShapeDtypeStruct((height, width, channels), BF16),
            jax.ShapeDtypeStruct((height, width, channels), F32),
        ),
        in_specs=[
            pl.BlockSpec((2, 2, width, channels), lambda s: (0, s, 0, 0)),
            vmem,
            pair_block(),
            vmem,
            vmem,
        ],
        out_specs=(pair_block(), pair_block()),
        scratch_shapes=[
            pltpu.VMEM((height + 2, width, 3 * channels), BF16),
        ],
        compiler_params=pltpu.CompilerParams(vmem_limit_bytes=60 * 1024 * 1024),
        name="back",
    )(firsts, factors, video, wtime, wide2)
    return next_video[None], predicted[None]


def solution(mesh):
    bands = P(("clips", "frames"), "rows", None, None)
    in_specs = (bands, P("clips"), P(), P(), P(), P(), P(), P())
    return jax.shard_map(
        functools.partial(body, mesh.shape["rows"]),
        mesh=mesh,
        in_specs=in_specs,
        out_specs=(bands, bands),
        check_vma=False,
    )
```
